32 devices in a mesh: grp: 4 (over y, x), line: 8 (over z, core).
Axes of the slice: x: 2, y: 2, z: 4, core: 2. Of those that a mesh axis runs over, the one named last changes fastest.
Arguments:
- adjoint: float32 [5, 16, 1024, 1024], P(None, 'grp', 'line'), may hold values from -6 to 6
- source: float32 [5, 16, 1024, 1024], P(None, 'grp', 'line'), may hold values from -6 to 6
- jacobian: float32 [3, 5, 5], replicated, may hold values from -2.5 to 2.5
- inverse_x: float32 [1024, 1024], replicated, may hold values from 0 to 3
- inverse_y: float32 [1024, 1024], replicated, may hold values from 0 to 3
- inverse_z: float32 [16, 16], replicated, may hold values from 0 to 3
Outputs:
- update: float32 [5, 16, 1024, 1024], P(None, 'grp', 'line')
The draws below stay inside these ranges and needn't reach their ends.
All inputs are finite; a program needn't handle non-finite values.
Results may differ from the reference program's by a relative error of at most 0.00011.
Values sent between devices are 32-bit elements; how exact they have to be, the bound alone decides.
A program may use at most 256 MiB of HBM per device.

```python
import math
import jax
import jax.numpy as jnp
from jax import lax

VARS = 5
NX = 1024
NY = 1024
NZ = 16


def kernel_matrix(key, count, reach, spread):
    places = jnp.arange(count, dtype=jnp.float32)
    spacing = jnp.abs(places[:, None] - places[None, :])
    noise = jax.random.uniform(key, (count, count), jnp.float32, 1.0 - spread, 1.0 + spread)
    return (jnp.exp(-spacing / reach) * noise + jnp.eye(count, dtype=jnp.float32)) / math.sqrt(reach)


def draw_inverse_x(key, part):
    spread = 0.5
    return kernel_matrix(key, NX, max(NX // 4, 1), spread)


def draw_inverse_y(key, part):
    spread = 0.5
    return kernel_matrix(key, NY, max(NY // 4, 1), spread)


def draw_inverse_z(key, part):
    spread = 0.5
    return kernel_matrix(key, NZ, max(NZ // 2, 1), spread)


def block_scale(own_key, dims, split, least, high):
    factor_of, own = 1.0, jax.random.fold_in(own_key, 6)
    for position, parts in split:
        heights = jnp.exp(jax.random.uniform(jax.random.fold_in(own, position), (parts,), jnp.float32, least / len(split), high / len(split)))
        factor_of = factor_of * jnp.repeat(heights, dims[position] // parts).reshape([-1 if axis == position else 1 for axis in range(len(dims))])
    return factor_of


def centred(own_key, extent, scale, most, shards=(), kind=jnp.bfloat16):
    result = jax.random.normal(own_key, extent, jnp.float32) * scale
    if len(shards) > 0:
        result = block_scale(own_key, extent, shards, -0.22, 0.18) * result
    return jnp.clip(result, min=-most, max=most).astype(kind)


def setup_inputs(seed: int = 0) -> dict:
    streams_of = jax.random.split(jax.random.key(seed), 7)
    adjoint = centred(streams_of[0], (VARS, NZ, NY, NX), 1.0, 6.0, ((1, 4), (2, 8)), jnp.float32)
    source = centred(streams_of[1], (VARS, NZ, NY, NX), 1.0, 6.0, ((1, 4), (2, 8)), jnp.float32)
    jacobian = centred(streams_of[2], (3, VARS, VARS), 0.4, 2.5, (), jnp.float32)
    inverse_x = draw_inverse_x(jax.random.fold_in(streams_of[6], 71), 0)
    inverse_y = draw_inverse_y(jax.random.fold_in(streams_of[6], 71), 0)
    inverse_z = draw_inverse_z(jax.random.fold_in(streams_of[6], 71), 0)
    return dict(adjoint=adjoint, source=source, jacobian=jacobian, inverse_x=inverse_x, inverse_y=inverse_y, inverse_z=inverse_z)


dissipation = 0.05
highest = lax.Precision.HIGHEST


def reference(adjoint, source, jacobian, inverse_x, inverse_y, inverse_z):
    padded = jnp.pad(adjoint, ((0, 0), (2, 2), (2, 2), (2, 2)))

    def window(step_z, step_y, step_x):
        return padded[:, 2 + step_z:2 + step_z + NZ, 2 + step_y:2 + step_y + NY, 2 + step_x:2 + step_x + NX]

    centre = window(0, 0, 0)
    residual = source
    units = ((1, 0, 0), (0, 1, 0), (0, 0, 1))
    for direction in range(3):
        step_z, step_y, step_x = units[direction]
        forward = window(step_z, step_y, step_x)
        backward = window(-step_z, -step_y, -step_x)
        far_forward = window(2 * step_z, 2 * step_y, 2 * step_x)
        far_backward = window(-2 * step_z, -2 * step_y, -2 * step_x)
        central = 0.5 * (forward - backward)
        fourth = far_forward - 4.0 * forward + 6.0 * centre - 4.0 * backward + far_backward
        residual = residual + jnp.einsum("wv,wzyx->vzyx", jacobian[direction], central, precision=highest) - dissipation * fourth
    swept_x = jnp.einsum("vzyx,px->vzyp", residual, inverse_x, precision=highest)
    swept_y = jnp.einsum("vzyx,py->vzpx", swept_x, inverse_y, precision=highest)
    return jnp.einsum("vzyx,pz->vpyx", swept_y, inverse_z, precision=highest)
```

```python
import functools

import jax
import jax.numpy as jnp
from jax import lax
from jax.experimental import pallas as pl
from jax.experimental.pallas import tpu as pltpu
from jax.sharding import PartitionSpec as P

dissipation = 0.05
highest = lax.Precision.HIGHEST


def padded_2(cells, sides, width):
    for axis, dim in sides:
        count = lax.axis_size(axis)
        ends = count - 1
        head = lax.slice_in_dim(cells, 0, width, axis=dim)
        tail = lax.slice_in_dim(cells, cells.shape[dim] - width, cells.shape[dim], axis=dim)
        cells = jnp.concatenate(
            [
                lax.ppermute(tail, axis, [(i, (i + 1) % count) for i in range(ends)]),
                cells,
                lax.ppermute(head, axis, [((i + 1) % count, i) for i in range(ends)]),
            ],
            axis=dim,
        )
    return cells


def shift_last(field, offset):
    if offset == 0:
        return field
    zeros = jnp.zeros(field.shape[:-1] + (abs(offset),), field.dtype)
    if offset > 0:
        return jnp.concatenate([field[..., offset:], zeros], axis=-1)
    return jnp.concatenate([zeros, field[..., :offset]], axis=-1)


def stencil_sum(padded, source, jacobian):
    components = source.shape[0]
    depth = source.shape[1]
    rows_local = source.shape[2]

    def window(step_z, step_y, step_x):
        inner = padded[:, 2 + step_z : 2 + step_z + depth, 2 + step_y : 2 + step_y + rows_local, :]
        return shift_last(inner, step_x)

    centre = window(0, 0, 0)
    units = ((1, 0, 0), (0, 1, 0), (0, 0, 1))
    damping = jnp.zeros_like(source)
    centrals = []
    for direction in range(3):
        step_z, step_y, step_x = units[direction]
        forward = window(step_z, step_y, step_x)
        backward = window(-step_z, -step_y, -step_x)
        far_forward = window(2 * step_z, 2 * step_y, 2 * step_x)
        far_backward = window(-2 * step_z, -2 * step_y, -2 * step_x)
        centrals.append(0.5 * (forward - backward))
        damping = damping + (
            far_forward - 4.0 * forward + 6.0 * centre - 4.0 * backward + far_backward
        )
    outputs = []
    for target in range(components):
        total = source[target]
        for direction in range(3):
            for anchor in range(components):
                total = total + jacobian[direction, anchor, target] * centrals[direction][anchor]
        outputs.append(total)
    return jnp.stack(outputs, axis=0) - dissipation * damping


def shards_plain(adjoint, source, jacobian, inverse_x, inverse_y, inverse_z):
    components = adjoint.shape[0]
    depth = adjoint.shape[1]
    rows_local = adjoint.shape[2]
    width = adjoint.shape[3]
    line_count = lax.axis_size("line")
    group_count = lax.axis_size("grp")
    total_y = inverse_y.shape[0]
    total_z = inverse_z.shape[0]
    padded = padded_2(adjoint, (("grp", 1), ("line", 2)), 2)
    residual = stencil_sum(padded, source, jacobian)
    flat = residual.reshape(components * depth * rows_local, width)
    swept = lax.dot_general(inverse_x, flat, (((1,), (1,)), ((), ())), precision=highest)
    block_x = width // line_count
    block_y = total_y // group_count
    sent = swept.reshape(line_count, block_x * components * depth * rows_local)
    lines = lax.all_to_all(sent, "line", split_axis=0, concat_axis=0, tiled=True)
    lines = lines.reshape(line_count, block_x * components * depth, rows_local)
    split_y = inverse_y.reshape(total_y, line_count, rows_local)
    along_y = lax.dot_general(lines, split_y, (((0, 2), (1, 2)), ((), ())), precision=highest)
    along_y = along_y.reshape(block_x * components, depth, group_count, block_y)
    columns = lax.all_to_all(along_y, "grp", split_axis=2, concat_axis=1, tiled=True)
    columns = columns.reshape(block_x * components, total_z, block_y)
    along_z = lax.dot_general(inverse_z, columns, (((1,), (1,)), ((), ())), precision=highest)
    regrouped = lax.all_to_all(along_z, "grp", split_axis=0, concat_axis=2, tiled=True)
    regrouped = regrouped.reshape(depth, block_x, components, line_count, rows_local)
    returned = lax.all_to_all(regrouped, "line", split_axis=3, concat_axis=1, tiled=True)
    returned = returned.reshape(depth, width, components, rows_local)
    return jnp.transpose(returned, (2, 0, 3, 1))


MESH = pl.DeviceIdType.MESH


def halves(values):
    high = values.astype(jnp.bfloat16)
    return high, (values - high.astype(jnp.float32)).astype(jnp.bfloat16)


def split_halves(values):
    high = lax.reduce_precision(values, exponent_bits=8, mantissa_bits=7)
    return high.astype(jnp.bfloat16), (values - high).astype(jnp.bfloat16)


def product(left, right):
    dims = (((1,), (1,)), ((), ()))

    def one(a, b):
        return lax.dot_general(a, b, dims, preferred_element_type=jnp.float32)

    return one(left[0], right[0]) + (one(left[0], right[1]) + one(left[1], right[0]))


def sweep_x_body(high_ref, low_ref, field_ref, out_ref):
    depth, rows, width = field_ref.shape[1:]
    field = halves(field_ref[0].reshape(depth * rows, width))
    swept = product((high_ref[...], low_ref[...]), field)
    for plane in range(depth):
        part = swept[:, plane * rows : (plane + 1) * rows]
        out_ref[0, :, plane] = part.reshape(out_ref.shape[1], out_ref.shape[3], rows)


def sweep_x(high, low, residual, devices):
    components, depth, rows, width = residual.shape
    columns = width // devices
    return pl.pallas_call(
        sweep_x_body,
        grid=(components,),
        in_specs=[
            pl.BlockSpec((width, width), lambda v: (0, 0)),
            pl.BlockSpec((width, width), lambda v: (0, 0)),
            pl.BlockSpec((1, depth, rows, width), lambda v: (v, 0, 0, 0)),
        ],
        out_specs=pl.BlockSpec((1, devices, depth, columns, rows), lambda v: (v, 0, 0, 0, 0)),
        out_shape=jax.ShapeDtypeStruct((components, devices, depth, columns, rows), jnp.float32),
        compiler_params=pltpu.CompilerParams(vmem_limit_bytes=48 * 2**20),
    )(high, low, residual)


def middle_body(
    groups, lines, z_ref, high_ref, low_ref, sent_ref, back_ref,
    got, done, field_high, field_low, lined, send_one, recv_one, send_two, recv_two,
):
    components, devices, depth, columns, rows = sent_ref.shape
    total_z = groups * depth
    own_g = lax.axis_index("grp")
    own_l = lax.axis_index("line")
    own = own_g * lines + own_l

    def partner(step):
        l = lax.rem(own_l + step // groups, lines)
        g = lax.rem(own_g + step % groups, groups)
        return g, l

    barrier = pltpu.get_barrier_semaphore()

    def greet(step, carry):
        g, l = partner(step)
        pl.semaphore_signal(barrier, inc=1, device_id=(g, l), device_id_type=MESH)
        return carry

    lax.fori_loop(1, devices, greet, 0)
    pl.semaphore_wait(barrier, devices - 1)

    def first(v, carry):
        pltpu.make_async_copy(sent_ref.at[v, own], got.at[v, own], recv_one.at[v]).start()

        def one(step, c):
            g, l = partner(step)
            pltpu.make_async_remote_copy(
                src_ref=sent_ref.at[v, g * lines + l],
                dst_ref=got.at[v, own],
                send_sem=send_one.at[v],
                recv_sem=recv_one.at[v],
                device_id=(g, l),
                device_id_type=MESH,
            ).start()
            return c

        lax.fori_loop(1, devices, one, 0)
        return carry

    lax.fori_loop(0, components, first, 0)

    def solve(v, carry):
        pltpu.make_async_copy(got.at[v], got.at[v], recv_one.at[v]).wait()
        for g in range(groups):
            block = jnp.concatenate(
                [got[v, g * lines + l].reshape(depth * columns, rows) for l in range(lines)], axis=-1
            )
            high, low = halves(block)
            field_high[pl.ds(g * depth * columns, depth * columns), :] = high
            field_low[pl.ds(g * depth * columns, depth * columns), :] = low

        def line(i, c):
            l = lax.rem(own_l + i, lines)
            at = pl.ds(pl.multiple_of(l * rows, rows), rows)
            solved = product(
                (field_high[...], field_low[...]), (high_ref[at, :], low_ref[at, :])
            )
            lined[...] = solved.reshape(total_z, columns, rows)
            for q in range(total_z):
                total = z_ref[q, 0] * lined[0]
                for z in range(1, total_z):
                    total = total + z_ref[q, z] * lined[z]
                done[v, (q // depth) * lines + l, q % depth] = total

            def send(j, cc):
                g = lax.rem(own_g + j, groups)
                pltpu.make_async_remote_copy(
                    src_ref=done.at[v, g * lines + l],
                    dst_ref=back_ref.at[v, own],
                    send_sem=send_two.at[v],
                    recv_sem=recv_two.at[v],
                    device_id=(g, l),
                    device_id_type=MESH,
                ).start()
                return cc

            @pl.when(i == 0)
            def _():
                pltpu.make_async_copy(done.at[v, own], back_ref.at[v, own], recv_two.at[v]).start()
                lax.fori_loop(1, groups, send, 0)

            @pl.when(i > 0)
            def _():
                lax.fori_loop(0, groups, send, 0)

            return c

        lax.fori_loop(0, lines, line, 0)
        return carry

    lax.fori_loop(0, components, solve, 0)

    def finish(v, carry):
        others = pl.ds(0, devices - 1)
        pltpu.make_async_copy(sent_ref.at[v, others], sent_ref.at[v, others], send_one.at[v]).wait()
        pltpu.make_async_copy(done.at[v, others], done.at[v, others], send_two.at[v]).wait()
        pltpu.make_async_copy(back_ref.at[v], back_ref.at[v], recv_two.at[v]).wait()
        return carry

    lax.fori_loop(0, components, finish, 0)


def middle(inverse_z, high, low, sent, groups, lines):
    components, devices, depth, columns, rows = sent.shape
    total_y = high.shape[0]
    total_z = groups * depth
    return pl.pallas_call(
        functools.partial(middle_body, groups, lines),
        in_specs=[
            pl.BlockSpec(memory_space=pltpu.SMEM),
            pl.BlockSpec(memory_space=pltpu.VMEM),
            pl.BlockSpec(memory_space=pltpu.VMEM),
            pl.BlockSpec(memory_space=pl.ANY),
        ],
        out_specs=pl.BlockSpec(memory_space=pl.ANY),
        out_shape=jax.ShapeDtypeStruct(sent.shape, jnp.float32),
        scratch_shapes=[
            pltpu.VMEM(sent.shape, jnp.float32),
            pltpu.VMEM(sent.shape, jnp.float32),
            pltpu.VMEM((total_z * columns, total_y), jnp.bfloat16),
            pltpu.VMEM((total_z * columns, total_y), jnp.bfloat16),
            pltpu.VMEM((total_z, columns, rows), jnp.float32),
            pltpu.SemaphoreType.DMA((components,)),
            pltpu.SemaphoreType.DMA((components,)),
            pltpu.SemaphoreType.DMA((components,)),
            pltpu.SemaphoreType.DMA((components,)),
        ],
        compiler_params=pltpu.CompilerParams(
            collective_id=0, has_side_effects=True, vmem_limit_bytes=48 * 2**20
        ),
    )(inverse_z, high, low, sent)


def turn_body(back_ref, out_ref):
    devices, depth, columns, rows = back_ref.shape[1:]
    for plane in range(depth):
        out_ref[0, plane] = back_ref[0, :, plane].reshape(devices * columns, rows).T


def turn(back):
    components, devices, depth, columns, rows = back.shape
    width = devices * columns
    return pl.pallas_call(
        turn_body,
        grid=(components,),
        in_specs=[pl.BlockSpec((1, devices, depth, columns, rows), lambda v: (v, 0, 0, 0, 0))],
        out_specs=pl.BlockSpec((1, depth, rows, width), lambda v: (v, 0, 0, 0)),
        out_shape=jax.ShapeDtypeStruct((components, depth, rows, width), jnp.float32),
        compiler_params=pltpu.CompilerParams(vmem_limit_bytes=32 * 2**20),
    )(back)


def shards_exchange(adjoint, source, jacobian, inverse_x, inverse_y, inverse_z):
    groups = lax.axis_size("grp")
    lines = lax.axis_size("line")
    padded = padded_2(adjoint, (("grp", 1), ("line", 2)), 2)
    residual = stencil_sum(padded, source, jacobian)
    sent = sweep_x(*split_halves(inverse_x), residual, groups * lines)
    back = middle(inverse_z, *split_halves(inverse_y), sent, groups, lines)
    return turn(back)


def shards(adjoint, source, jacobian, inverse_x, inverse_y, inverse_z):
    devices = lax.axis_size("grp") * lax.axis_size("line")
    whole_tiles = adjoint.shape[2] % 128 == 0 and (adjoint.shape[3] // devices) % 16 == 0
    chosen = shards_exchange if whole_tiles else shards_plain
    return chosen(adjoint, source, jacobian, inverse_x, inverse_y, inverse_z)


def solution(mesh):
    placed = (P(None, "grp", "line", None), P(None, "grp", "line", None), P(), P(), P(), P())
    return jax.shard_map(
        shards, mesh=mesh, in_specs=placed, out_specs=P(None, "grp", "line", None), check_vma=False
    )
```

```python
import functools

import jax
import jax.numpy as jnp
from jax import lax
from jax.experimental import pallas as pl
from jax.experimental.pallas import tpu as pltpu
from jax.sharding import PartitionSpec as P

dissipation = 0.05
highest = lax.Precision.HIGHEST


def padded_2(cells, sides, width):
    for axis, dim in sides:
        count = lax.axis_size(axis)
        ends = count - 1
        head = lax.slice_in_dim(cells, 0, width, axis=dim)
        tail = lax.slice_in_dim(cells, cells.shape[dim] - width, cells.shape[dim], axis=dim)
        cells = jnp.concatenate(
            [
                lax.ppermute(tail, axis, [(i, (i + 1) % count) for i in range(ends)]),
                cells,
                lax.ppermute(head, axis, [((i + 1) % count, i) for i in range(ends)]),
            ],
            axis=dim,
        )
    return cells


def shift_last(field, offset):
    if offset == 0:
        return field
    zeros = jnp.zeros(field.shape[:-1] + (abs(offset),), field.dtype)
    if offset > 0:
        return jnp.concatenate([field[..., offset:], zeros], axis=-1)
    return jnp.concatenate([zeros, field[..., :offset]], axis=-1)


def stencil_sum(padded, source, jacobian):
    components = source.shape[0]
    depth = source.shape[1]
    rows_local = source.shape[2]

    def window(step_z, step_y, step_x):
        inner = padded[:, 2 + step_z : 2 + step_z + depth, 2 + step_y : 2 + step_y + rows_local, :]
        return shift_last(inner, step_x)

    centre = window(0, 0, 0)
    units = ((1, 0, 0), (0, 1, 0), (0, 0, 1))
    damping = jnp.zeros_like(source)
    centrals = []
    for direction in range(3):
        step_z, step_y, step_x = units[direction]
        forward = window(step_z, step_y, step_x)
        backward = window(-step_z, -step_y, -step_x)
        far_forward = window(2 * step_z, 2 * step_y, 2 * step_x)
        far_backward = window(-2 * step_z, -2 * step_y, -2 * step_x)
        centrals.append(0.5 * (forward - backward))
        damping = damping + (
            far_forward - 4.0 * forward + 6.0 * centre - 4.0 * backward + far_backward
        )
    outputs = []
    for target in range(components):
        total = source[target]
        for direction in range(3):
            for anchor in range(components):
                total = total + jacobian[direction, anchor, target] * centrals[direction][anchor]
        outputs.append(total)
    return jnp.stack(outputs, axis=0) - dissipation * damping


def shards_plain(adjoint, source, jacobian, inverse_x, inverse_y, inverse_z):
    components = adjoint.shape[0]
    depth = adjoint.shape[1]
    rows_local = adjoint.shape[2]
    width = adjoint.shape[3]
    line_count = lax.axis_size("line")
    group_count = lax.axis_size("grp")
    total_y = inverse_y.shape[0]
    total_z = inverse_z.shape[0]
    padded = padded_2(adjoint, (("grp", 1), ("line", 2)), 2)
    residual = stencil_sum(padded, source, jacobian)
    flat = residual.reshape(components * depth * rows_local, width)
    swept = lax.dot_general(inverse_x, flat, (((1,), (1,)), ((), ())), precision=highest)
    block_x = width // line_count
    block_y = total_y // group_count
    sent = swept.reshape(line_count, block_x * components * depth * rows_local)
    lines = lax.all_to_all(sent, "line", split_axis=0, concat_axis=0, tiled=True)
    lines = lines.reshape(line_count, block_x * components * depth, rows_local)
    split_y = inverse_y.reshape(total_y, line_count, rows_local)
    along_y = lax.dot_general(lines, split_y, (((0, 2), (1, 2)), ((), ())), precision=highest)
    along_y = along_y.reshape(block_x * components, depth, group_count, block_y)
    columns = lax.all_to_all(along_y, "grp", split_axis=2, concat_axis=1, tiled=True)
    columns = columns.reshape(block_x * components, total_z, block_y)
    along_z = lax.dot_general(inverse_z, columns, (((1,), (1,)), ((), ())), precision=highest)
    regrouped = lax.all_to_all(along_z, "grp", split_axis=0, concat_axis=2, tiled=True)
    regrouped = regrouped.reshape(depth, block_x, components, line_count, rows_local)
    returned = lax.all_to_all(regrouped, "line", split_axis=3, concat_axis=1, tiled=True)
    returned = returned.reshape(depth, width, components, rows_local)
    return jnp.transpose(returned, (2, 0, 3, 1))


MESH = pl.DeviceIdType.MESH


def halves(values):
    high = values.astype(jnp.bfloat16)
    return high, (values - high.astype(jnp.float32)).astype(jnp.bfloat16)


def split_halves(values):
    high = lax.reduce_precision(values, exponent_bits=8, mantissa_bits=7)
    return high.astype(jnp.bfloat16), (values - high).astype(jnp.bfloat16)


def product(left, right):
    dims = (((1,), (1,)), ((), ()))

    def one(a, b):
        return lax.dot_general(a, b, dims, preferred_element_type=jnp.float32)

    return one(left[0], right[0]) + (one(left[0], right[1]) + one(left[1], right[0]))


def shift_x(field, offset, place):
    width = field.shape[-1]
    moved = pltpu.roll(field, (-offset) % width, axis=1)
    inside = place < width - offset if offset > 0 else place >= -offset
    return jnp.where(inside, moved, 0.0)


def residual_sweep_body(
    jacobian_ref, high_ref, low_ref, source_ref, cells_ref, below_ref, above_ref, before_ref, after_ref,
    out_ref, padded, residual, sems,
):
    v = pl.program_id(0)
    components = cells_ref.shape[0]
    depth, rows, width = source_ref.shape[1:]

    @pl.when(v == 0)
    def _():
        inner = pl.ds(2, depth)
        middle_rows = pl.ds(8, rows)
        copies = [
            pltpu.make_async_copy(cells_ref, padded.at[:, inner, middle_rows], sems.at[0]),
            pltpu.make_async_copy(below_ref, padded.at[:, pl.ds(0, 2), middle_rows], sems.at[1]),
            pltpu.make_async_copy(above_ref, padded.at[:, pl.ds(depth + 2, 2), middle_rows], sems.at[2]),
            pltpu.make_async_copy(before_ref, padded.at[:, inner, pl.ds(0, 8)], sems.at[3]),
            pltpu.make_async_copy(after_ref, padded.at[:, inner, pl.ds(rows + 8, 8)], sems.at[4]),
        ]
        for copy in copies:
            copy.start()
        for copy in copies:
            copy.wait()

    place = lax.broadcasted_iota(jnp.int32, (8, width), 1)
    row = lax.broadcasted_iota(jnp.int32, (8, width), 0)
    factors = [[0.5 * jacobian_ref[d, w, v] for w in range(components)] for d in range(3)]

    def plane(z):
        def read(w, dz, start):
            return padded[w, z + 2 + dz, pl.ds(start, 8), :]

        def along(start):
            total = factors[1][0] * read(0, 0, start)
            for w in range(1, components):
                total = total + factors[1][w] * read(w, 0, start)
            return total

        def tile(t, carry):
            behind, here = carry
            start = pl.multiple_of(t * 8, 8)
            at = pl.multiple_of(t * 8 + 8, 8)
            after = pl.multiple_of(t * 8 + 16, 8)
            ahead = along(after)
            total = source_ref[0, z, pl.ds(start, 8), :]
            across = factors[2][0] * read(0, 0, at)
            for w in range(1, components):
                across = across + factors[2][w] * read(w, 0, at)
            for w in range(components):
                total = total + factors[0][w] * (read(w, 1, at) - read(w, -1, at))
            centre, last, coming = read(v, 0, at), read(v, 0, start), read(v, 0, after)
            scale = 4.0 * dissipation
            total = total + scale * (read(v, 1, at) + read(v, -1, at))
            scaled = scale * centre
            forward = jnp.where(row == 0, scale * coming + ahead, scaled + here)
            backward = jnp.where(row == 7, scale * last - behind, scaled - here)
            total = total + pltpu.roll(forward, 7, axis=0) + pltpu.roll(backward, 1, axis=0)
            total = total + shift_x(scaled + across, 1, place) + shift_x(scaled - across, -1, place)
            far = read(v, 2, at) + read(v, -2, at)
            far = far + pltpu.roll(jnp.where(row < 2, coming, centre), 6, axis=0)
            far = far + pltpu.roll(jnp.where(row >= 6, last, centre), 2, axis=0)
            far = far + shift_x(centre, 2, place) + shift_x(centre, -2, place)
            total = total - dissipation * (far + 18.0 * centre)
            residual[pl.ds(pl.multiple_of(z * rows + start, 8), 8), :] = total
            return here, ahead

        lax.fori_loop(0, rows // 8, tile, (along(0), along(8)))

    for z in range(depth):
        plane(z)
    swept = product((high_ref[...], low_ref[...]), halves(residual[...]))
    for plane in range(depth):
        part = swept[:, plane * rows : (plane + 1) * rows]
        out_ref[0, :, plane] = part.reshape(out_ref.shape[1], out_ref.shape[3], rows)


def residual_sweep(jacobian, high, low, source, cells, rims, devices):
    components, depth, rows, width = source.shape
    columns = width // devices
    once = pl.Buffered(1)
    return pl.pallas_call(
        residual_sweep_body,
        grid=(components,),
        in_specs=[
            pl.BlockSpec(memory_space=pltpu.SMEM),
            pl.BlockSpec((width, width), lambda v: (0, 0), pipeline_mode=once),
            pl.BlockSpec((width, width), lambda v: (0, 0), pipeline_mode=once),
            pl.BlockSpec((1, depth, rows, width), lambda v: (v, 0, 0, 0)),
        ]
        + [pl.BlockSpec(memory_space=pl.ANY)] * 5,
        out_specs=pl.BlockSpec((1, devices, depth, columns, rows), lambda v: (v, 0, 0, 0, 0)),
        out_shape=jax.ShapeDtypeStruct((components, devices, depth, columns, rows), jnp.float32),
        scratch_shapes=[
            pltpu.VMEM((components, depth + 4, rows + 16, width), jnp.float32),
            pltpu.VMEM((depth * rows, width), jnp.float32),
            pltpu.SemaphoreType.DMA((5,)),
        ],
        compiler_params=pltpu.CompilerParams(vmem_limit_bytes=56 * 2**20),
    )(jacobian, high, low, source, cells, *rims)


def rims_of(cells):
    rims = []
    for axis, dim, width in (("grp", 1, 2), ("line", 2, 8)):
        count = lax.axis_size(axis)
        size = cells.shape[dim]
        head = lax.slice_in_dim(cells, 0, width, axis=dim)
        tail = lax.slice_in_dim(cells, size - width, size, axis=dim)
        if axis == "grp" and count == 4:
            rims.append(relayed(tail, ((0, 1), (2, 3)), (1, 3, 2)))
            rims.append(relayed(head, ((1, 0), (3, 2)), (2, 0, 1)))
        else:
            rims.append(lax.ppermute(tail, axis, [(i, i + 1) for i in range(count - 1)]))
            rims.append(lax.ppermute(head, axis, [(i + 1, i) for i in range(count - 1)]))
    return rims


def relayed(rim, near, route):
    first, corner, last = route
    half = rim.shape[-1] // 2
    direct = lax.ppermute(rim[..., :half], "grp", [*near, (first, last)])
    side = lax.ppermute(rim[..., half:], "grp", [(first, corner)])
    rest = lax.ppermute(rim[..., half:], "grp", list(near))
    side = lax.ppermute(side, "grp", [(corner, last)])
    mine = lax.axis_index("grp") == last
    return jnp.concatenate([direct, jnp.where(mine, side, rest)], axis=-1)


def middle_body(
    groups, lines, z_ref, high_ref, low_ref, sent_ref, back_ref,
    got, done, field_high, field_low, lined, send_one, recv_one, send_two, recv_two,
):
    components, devices, depth, columns, rows = sent_ref.shape
    total_z = groups * depth
    own_g = lax.axis_index("grp")
    own_l = lax.axis_index("line")
    own = own_g * lines + own_l

    def partner(step):
        l = lax.rem(own_l + step // groups, lines)
        g = lax.rem(own_g + step % groups, groups)
        return g, l

    barrier = pltpu.get_barrier_semaphore()

    def greet(step, carry):
        g, l = partner(step)
        pl.semaphore_signal(barrier, inc=1, device_id=(g, l), device_id_type=MESH)
        return carry

    lax.fori_loop(1, devices, greet, 0)
    pl.semaphore_wait(barrier, devices - 1)

    def first(v, carry):
        pltpu.make_async_copy(sent_ref.at[v, own], got.at[v, own], recv_one.at[v]).start()

        def one(step, c):
            g, l = partner(step)
            pltpu.make_async_remote_copy(
                src_ref=sent_ref.at[v, g * lines + l],
                dst_ref=got.at[v, own],
                send_sem=send_one.at[v],
                recv_sem=recv_one.at[v],
                device_id=(g, l),
                device_id_type=MESH,
            ).start()
            return c

        lax.fori_loop(1, devices, one, 0)
        return carry

    lax.fori_loop(0, components, first, 0)

    def solve(v, carry):
        pltpu.make_async_copy(got.at[v], got.at[v], recv_one.at[v]).wait()
        for g in range(groups):
            block = jnp.concatenate(
                [got[v, g * lines + l].reshape(depth * columns, rows) for l in range(lines)], axis=-1
            )
            high, low = halves(block)
            field_high[pl.ds(g * depth * columns, depth * columns), :] = high
            field_low[pl.ds(g * depth * columns, depth * columns), :] = low

        def line(i, c):
            l = lax.rem(own_l + i, lines)
            at = pl.ds(pl.multiple_of(l * rows, rows), rows)
            solved = product(
                (field_high[...], field_low[...]), (high_ref[at, :], low_ref[at, :])
            )
            lined[...] = solved.reshape(total_z, columns, rows)
            for q in range(total_z):
                total = z_ref[q, 0] * lined[0]
                for z in range(1, total_z):
                    total = total + z_ref[q, z] * lined[z]
                done[v, (q // depth) * lines + l, q % depth] = total

            def send(j, cc):
                g = lax.rem(own_g + j, groups)
                pltpu.make_async_remote_copy(
                    src_ref=done.at[v, g * lines + l],
                    dst_ref=back_ref.at[v, own],
                    send_sem=send_two.at[v],
                    recv_sem=recv_two.at[v],
                    device_id=(g, l),
                    device_id_type=MESH,
                ).start()
                return cc

            @pl.when(i == 0)
            def _():
                pltpu.make_async_copy(done.at[v, own], back_ref.at[v, own], recv_two.at[v]).start()
                lax.fori_loop(1, groups, send, 0)

            @pl.when(i > 0)
            def _():
                lax.fori_loop(0, groups, send, 0)

            return c

        lax.fori_loop(0, lines, line, 0)
        return carry

    lax.fori_loop(0, components, solve, 0)

    def finish(v, carry):
        others = pl.ds(0, devices - 1)
        pltpu.make_async_copy(sent_ref.at[v, others], sent_ref.at[v, others], send_one.at[v]).wait()
        pltpu.make_async_copy(done.at[v, others], done.at[v, others], send_two.at[v]).wait()
        pltpu.make_async_copy(back_ref.at[v], back_ref.at[v], recv_two.at[v]).wait()
        return carry

    lax.fori_loop(0, components, finish, 0)


def middle(inverse_z, high, low, sent, groups, lines):
    components, devices, depth, columns, rows = sent.shape
    total_y = high.shape[0]
    total_z = groups * depth
    return pl.pallas_call(
        functools.partial(middle_body, groups, lines),
        in_specs=[
            pl.BlockSpec(memory_space=pltpu.SMEM),
            pl.BlockSpec(memory_space=pltpu.VMEM),
            pl.BlockSpec(memory_space=pltpu.VMEM),
            pl.BlockSpec(memory_space=pl.ANY),
        ],
        out_specs=pl.BlockSpec(memory_space=pl.ANY),
        out_shape=jax.ShapeDtypeStruct(sent.shape, jnp.float32),
        scratch_shapes=[
            pltpu.VMEM(sent.shape, jnp.float32),
            pltpu.VMEM(sent.shape, jnp.float32),
            pltpu.VMEM((total_z * columns, total_y), jnp.bfloat16),
            pltpu.VMEM((total_z * columns, total_y), jnp.bfloat16),
            pltpu.VMEM((total_z, columns, rows), jnp.float32),
            pltpu.SemaphoreType.DMA((components,)),
            pltpu.SemaphoreType.DMA((components,)),
            pltpu.SemaphoreType.DMA((components,)),
            pltpu.SemaphoreType.DMA((components,)),
        ],
        compiler_params=pltpu.CompilerParams(
            collective_id=0, has_side_effects=True, vmem_limit_bytes=48 * 2**20
        ),
    )(inverse_z, high, low, sent)


def turn_body(back_ref, out_ref):
    devices, depth, columns, rows = back_ref.shape[1:]
    for plane in range(depth):
        out_ref[0, plane] = back_ref[0, :, plane].reshape(devices * columns, rows).T


def turn(back):
    components, devices, depth, columns, rows = back.shape
    width = devices * columns
    return pl.pallas_call(
        turn_body,
        grid=(components,),
        in_specs=[pl.BlockSpec((1, devices, depth, columns, rows), lambda v: (v, 0, 0, 0, 0))],
        out_specs=pl.BlockSpec((1, depth, rows, width), lambda v: (v, 0, 0, 0)),
        out_shape=jax.ShapeDtypeStruct((components, depth, rows, width), jnp.float32),
        compiler_params=pltpu.CompilerParams(vmem_limit_bytes=32 * 2**20),
    )(back)


def shards_exchange(adjoint, source, jacobian, inverse_x, inverse_y, inverse_z):
    groups = lax.axis_size("grp")
    lines = lax.axis_size("line")
    rims = rims_of(adjoint)
    sent = residual_sweep(
        jacobian, *split_halves(inverse_x), source, adjoint, rims, groups * lines
    )
    back = middle(inverse_z, *split_halves(inverse_y), sent, groups, lines)
    return turn(back)


def shards(adjoint, source, jacobian, inverse_x, inverse_y, inverse_z):
    devices = lax.axis_size("grp") * lax.axis_size("line")
    whole_tiles = adjoint.shape[2] % 128 == 0 and (adjoint.shape[3] // devices) % 16 == 0
    chosen = shards_exchange if whole_tiles else shards_plain
    return chosen(adjoint, source, jacobian, inverse_x, inverse_y, inverse_z)


def solution(mesh):
    placed = (P(None, "grp", "line", None), P(None, "grp", "line", None), P(), P(), P(), P())
    return jax.shard_map(
        shards, mesh=mesh, in_specs=placed, out_specs=P(None, "grp", "line", None), check_vma=False
    )
```

```python
import functools

import jax
import jax.numpy as jnp
from jax import lax
from jax.experimental import pallas as pl
from jax.experimental.pallas import tpu as pltpu
from jax.sharding import PartitionSpec as P

dissipation = 0.05
highest = lax.Precision.HIGHEST


def padded_2(cells, sides, width):
    for axis, dim in sides:
        count = lax.axis_size(axis)
        ends = count - 1
        head = lax.slice_in_dim(cells, 0, width, axis=dim)
        tail = lax.slice_in_dim(cells, cells.shape[dim] - width, cells.shape[dim], axis=dim)
        cells = jnp.concatenate(
            [
                lax.ppermute(tail, axis, [(i, (i + 1) % count) for i in range(ends)]),
                cells,
                lax.ppermute(head, axis, [((i + 1) % count, i) for i in range(ends)]),
            ],
            axis=dim,
        )
    return cells


def shift_last(field, offset):
    if offset == 0:
        return field
    zeros = jnp.zeros(field.shape[:-1] + (abs(offset),), field.dtype)
    if offset > 0:
        return jnp.concatenate([field[..., offset:], zeros], axis=-1)
    return jnp.concatenate([zeros, field[..., :offset]], axis=-1)


def stencil_sum(padded, source, jacobian):
    components = source.shape[0]
    depth = source.shape[1]
    rows_local = source.shape[2]

    def window(step_z, step_y, step_x):
        inner = padded[:, 2 + step_z : 2 + step_z + depth, 2 + step_y : 2 + step_y + rows_local, :]
        return shift_last(inner, step_x)

    centre = window(0, 0, 0)
    units = ((1, 0, 0), (0, 1, 0), (0, 0, 1))
    damping = jnp.zeros_like(source)
    centrals = []
    for direction in range(3):
        step_z, step_y, step_x = units[direction]
        forward = window(step_z, step_y, step_x)
        backward = window(-step_z, -step_y, -step_x)
        far_forward = window(2 * step_z, 2 * step_y, 2 * step_x)
        far_backward = window(-2 * step_z, -2 * step_y, -2 * step_x)
        centrals.append(0.5 * (forward - backward))
        damping = damping + (
            far_forward - 4.0 * forward + 6.0 * centre - 4.0 * backward + far_backward
        )
    outputs = []
    for target in range(components):
        total = source[target]
        for direction in range(3):
            for anchor in range(components):
                total = total + jacobian[direction, anchor, target] * centrals[direction][anchor]
        outputs.append(total)
    return jnp.stack(outputs, axis=0) - dissipation * damping


def shards_plain(adjoint, source, jacobian, inverse_x, inverse_y, inverse_z):
    components = adjoint.shape[0]
    depth = adjoint.shape[1]
    rows_local = adjoint.shape[2]
    width = adjoint.shape[3]
    line_count = lax.axis_size("line")
    group_count = lax.axis_size("grp")
    total_y = inverse_y.shape[0]
    total_z = inverse_z.shape[0]
    padded = padded_2(adjoint, (("grp", 1), ("line", 2)), 2)
    residual = stencil_sum(padded, source, jacobian)
    flat = residual.reshape(components * depth * rows_local, width)
    swept = lax.dot_general(inverse_x, flat, (((1,), (1,)), ((), ())), precision=highest)
    block_x = width // line_count
    block_y = total_y // group_count
    sent = swept.reshape(line_count, block_x * components * depth * rows_local)
    lines = lax.all_to_all(sent, "line", split_axis=0, concat_axis=0, tiled=True)
    lines = lines.reshape(line_count, block_x * components * depth, rows_local)
    split_y = inverse_y.reshape(total_y, line_count, rows_local)
    along_y = lax.dot_general(lines, split_y, (((0, 2), (1, 2)), ((), ())), precision=highest)
    along_y = along_y.reshape(block_x * components, depth, group_count, block_y)
    columns = lax.all_to_all(along_y, "grp", split_axis=2, concat_axis=1, tiled=True)
    columns = columns.reshape(block_x * components, total_z, block_y)
    along_z = lax.dot_general(inverse_z, columns, (((1,), (1,)), ((), ())), precision=highest)
    regrouped = lax.all_to_all(along_z, "grp", split_axis=0, concat_axis=2, tiled=True)
    regrouped = regrouped.reshape(depth, block_x, components, line_count, rows_local)
    returned = lax.all_to_all(regrouped, "line", split_axis=3, concat_axis=1, tiled=True)
    returned = returned.reshape(depth, width, components, rows_local)
    return jnp.transpose(returned, (2, 0, 3, 1))


MESH = pl.DeviceIdType.MESH


def halves(values):
    high = values.astype(jnp.bfloat16)
    return high, (values - high.astype(jnp.float32)).astype(jnp.bfloat16)


def split_halves(values):
    high = lax.reduce_precision(values, exponent_bits=8, mantissa_bits=7)
    return high.astype(jnp.bfloat16), (values - high).astype(jnp.bfloat16)


def product(left, right):
    dims = (((1,), (1,)), ((), ()))

    def one(a, b):
        return lax.dot_general(a, b, dims, preferred_element_type=jnp.float32)

    return one(left[0], right[0]) + (one(left[0], right[1]) + one(left[1], right[0]))


def shift_x(field, offset, place):
    width = field.shape[-1]
    moved = pltpu.roll(field, (-offset) % width, axis=1)
    inside = place < width - offset if offset > 0 else place >= -offset
    return jnp.where(inside, moved, 0.0)


def residual_sweep_body(
    pair, jacobian_ref, high_ref, low_ref, source_ref, first_ref, second_ref, before_ref, after_ref, *rest

):
    out_ref, padded, residual, sems = rest[-4:]
    v = pl.program_id(0)
    components = first_ref.shape[0]
    depth, rows, width = source_ref.shape[1:]

    @pl.when(v == 0)
    def _():
        inner = pl.ds(2, depth)
        middle_rows = pl.ds(8, rows)
        cut = first_ref.shape[1]
        copies = [
            pltpu.make_async_copy(first_ref, padded.at[:, pl.ds(0, cut), middle_rows], sems.at[0]),
            pltpu.make_async_copy(
                second_ref, padded.at[:, pl.ds(cut, depth + 4 - cut), middle_rows], sems.at[1]
            ),
            pltpu.make_async_copy(
                before_ref.at[:, pl.ds(pair * depth, depth)], padded.at[:, inner, pl.ds(0, 8)], sems.at[2]
            ),
            pltpu.make_async_copy(
                after_ref.at[:, pl.ds(pair * depth, depth)],
                padded.at[:, inner, pl.ds(rows + 8, 8)],
                sems.at[3],
            ),
        ]
        for copy in copies:
            copy.start()
        for copy in copies:
            copy.wait()

    place = lax.broadcasted_iota(jnp.int32, (8, width), 1)
    row = lax.broadcasted_iota(jnp.int32, (8, width), 0)
    factors = [[0.5 * jacobian_ref[d, w, v] for w in range(components)] for d in range(3)]

    def plane(z):
        def read(w, dz, start):
            return padded[w, z + 2 + dz, pl.ds(start, 8), :]

        def along(start):
            total = factors[1][0] * read(0, 0, start)
            for w in range(1, components):
                total = total + factors[1][w] * read(w, 0, start)
            return total

        def tile(t, carry):
            behind, here = carry
            start = pl.multiple_of(t * 8, 8)
            at = pl.multiple_of(t * 8 + 8, 8)
            after = pl.multiple_of(t * 8 + 16, 8)
            ahead = along(after)
            total = source_ref[0, z, pl.ds(start, 8), :]
            across = factors[2][0] * read(0, 0, at)
            for w in range(1, components):
                across = across + factors[2][w] * read(w, 0, at)
            for w in range(components):
                total = total + factors[0][w] * (read(w, 1, at) - read(w, -1, at))
            centre, last, coming = read(v, 0, at), read(v, 0, start), read(v, 0, after)
            scale = 4.0 * dissipation
            total = total + scale * (read(v, 1, at) + read(v, -1, at))
            scaled = scale * centre
            forward = jnp.where(row == 0, scale * coming + ahead, scaled + here)
            backward = jnp.where(row == 7, scale * last - behind, scaled - here)
            total = total + pltpu.roll(forward, 7, axis=0) + pltpu.roll(backward, 1, axis=0)
            total = total + shift_x(scaled + across, 1, place) + shift_x(scaled - across, -1, place)
            far = read(v, 2, at) + read(v, -2, at)
            far = far + pltpu.roll(jnp.where(row < 2, coming, centre), 6, axis=0)
            far = far + pltpu.roll(jnp.where(row >= 6, last, centre), 2, axis=0)
            far = far + shift_x(centre, 2, place) + shift_x(centre, -2, place)
            total = total - dissipation * (far + 18.0 * centre)
            residual[pl.ds(pl.multiple_of(z * rows + start, 8), 8), :] = total
            return here, ahead

        lax.fori_loop(0, rows // 8, tile, (along(0), along(8)))

    for z in range(depth):
        plane(z)
    swept = product((high_ref[...], low_ref[...]), halves(residual[...]))
    for plane in range(depth):
        part = swept[:, plane * rows : (plane + 1) * rows]
        out_ref[0, :, plane] = part.reshape(out_ref.shape[1], out_ref.shape[3], rows)


def residual_sweep(pair, jacobian, high, low, source, parts, ahead, devices):
    components, depth, rows, width = source.shape
    depth = depth // 2
    columns = width // devices
    once = pl.Buffered(1)
    return pl.pallas_call(
        functools.partial(residual_sweep_body, pair),
        grid=(components,),
        in_specs=[
            pl.BlockSpec(memory_space=pltpu.SMEM),
            pl.BlockSpec((width, width), lambda v: (0, 0), pipeline_mode=once),
            pl.BlockSpec((width, width), lambda v: (0, 0), pipeline_mode=once),
            pl.BlockSpec((1, depth, rows, width), lambda v: (v, pair, 0, 0)),
        ]
        + [pl.BlockSpec(memory_space=pl.ANY)] * (len(parts) + len(ahead)),
        out_specs=pl.BlockSpec((1, devices, depth, columns, rows), lambda v: (v, 0, 0, 0, 0)),
        out_shape=jax.ShapeDtypeStruct((components, devices, depth, columns, rows), jnp.float32),
        scratch_shapes=[
            pltpu.VMEM((components, depth + 4, rows + 16, width), jnp.float32),
            pltpu.VMEM((depth * rows, width), jnp.float32),
            pltpu.SemaphoreType.DMA((4,)),
        ],
        compiler_params=pltpu.CompilerParams(vmem_limit_bytes=48 * 2**20),
    )(jacobian, high, low, source, *parts, *ahead)


def meet(groups, lines):
    devices = groups * lines
    own_g = lax.axis_index("grp")
    own_l = lax.axis_index("line")

    def partner(step):
        l = lax.rem(own_l + step // groups, lines)
        g = lax.rem(own_g + step % groups, groups)
        return g, l

    barrier = pltpu.get_barrier_semaphore()

    def greet(step, carry):
        g, l = partner(step)
        pl.semaphore_signal(barrier, inc=1, device_id=(g, l), device_id_type=MESH)
        return carry

    lax.fori_loop(1, devices, greet, 0)
    pl.semaphore_wait(barrier, devices - 1)
    return own_g, own_l, partner


def spread_body(groups, lines, sent_ref, got_ref, send_sem, recv_sem):
    components, devices = sent_ref.shape[:2]
    own_g, own_l, partner = meet(groups, lines)
    own = own_g * lines + own_l
    pltpu.make_async_copy(sent_ref.at[:, own], got_ref.at[:, own], recv_sem).start()

    def one(step, c):
        g, l = partner(step)
        pltpu.make_async_remote_copy(
            src_ref=sent_ref.at[:, g * lines + l],
            dst_ref=got_ref.at[:, own],
            send_sem=send_sem,
            recv_sem=recv_sem,
            device_id=(g, l),
            device_id_type=MESH,
        ).start()
        return c

    lax.fori_loop(1, devices, one, 0)
    others = pl.ds(0, devices - 1)
    pltpu.make_async_copy(sent_ref.at[:, others], sent_ref.at[:, others], send_sem).wait()
    pltpu.make_async_copy(got_ref, got_ref, recv_sem).wait()


def spread(sent, groups, lines):
    return pl.pallas_call(
        functools.partial(spread_body, groups, lines),
        in_specs=[pl.BlockSpec(memory_space=pl.ANY)],
        out_specs=pl.BlockSpec(memory_space=pl.ANY),
        out_shape=jax.ShapeDtypeStruct(sent.shape, jnp.float32),
        scratch_shapes=[pltpu.SemaphoreType.DMA, pltpu.SemaphoreType.DMA],
        cost_estimate=pl.CostEstimate(
            flops=10**11, bytes_accessed=2 * sent.size * 4, transcendentals=0
        ),
        compiler_params=pltpu.CompilerParams(collective_id=1, has_side_effects=True),
    )(sent)


def middle_body(
    groups, lines, z_ref, high_ref, low_ref, early_ref, sent_ref, back_ref,
    early, got, done, field_high, field_low, lined, early_sem, send_one, recv_one, send_two, recv_two,
):
    components, devices, depth, columns, rows = sent_ref.shape
    total_z = groups * 2 * depth
    own_g, own_l, partner = meet(groups, lines)
    own = own_g * lines + own_l
    fetch = pltpu.make_async_copy(early_ref, early, early_sem)
    fetch.start()

    def first(v, carry):
        pltpu.make_async_copy(sent_ref.at[v, own], got.at[v, own], recv_one.at[v]).start()

        def one(step, c):
            g, l = partner(step)
            pltpu.make_async_remote_copy(
                src_ref=sent_ref.at[v, g * lines + l],
                dst_ref=got.at[v, own],
                send_sem=send_one.at[v],
                recv_sem=recv_one.at[v],
                device_id=(g, l),
                device_id_type=MESH,
            ).start()
            return c

        lax.fori_loop(1, devices, one, 0)
        return carry

    lax.fori_loop(0, components, first, 0)
    fetch.wait()

    def solve(v, carry):
        pltpu.make_async_copy(got.at[v], got.at[v], recv_one.at[v]).wait()
        for g in range(groups):
            for place, half in enumerate((early, got)):
                block = jnp.concatenate(
                    [half[v, g * lines + l].reshape(depth * columns, rows) for l in range(lines)],
                    axis=-1,
                )
                high, low = halves(block)
                at = pl.ds((2 * g + place) * depth * columns, depth * columns)
                field_high[at, :] = high
                field_low[at, :] = low

        def line(i, c):
            l = lax.rem(own_l + i, lines)
            at = pl.ds(pl.multiple_of(l * rows, rows), rows)
            solved = product(
                (field_high[...], field_low[...]), (high_ref[at, :], low_ref[at, :])
            )
            lined[...] = solved.reshape(total_z, columns, rows)
            for q in range(total_z):
                total = z_ref[q, 0] * lined[0]
                for z in range(1, total_z):
                    total = total + z_ref[q, z] * lined[z]
                done[v, (q // (2 * depth)) * lines + l, q % (2 * depth)] = total

            def send(j, cc):
                g = lax.rem(own_g + j, groups)
                pltpu.make_async_remote_copy(
                    src_ref=done.at[v, g * lines + l],
                    dst_ref=back_ref.at[v, own],
                    send_sem=send_two.at[v],
                    recv_sem=recv_two.at[v],
                    device_id=(g, l),
                    device_id_type=MESH,
                ).start()
                return cc

            @pl.when(i == 0)
            def _():
                pltpu.make_async_copy(done.at[v, own], back_ref.at[v, own], recv_two.at[v]).start()
                lax.fori_loop(1, groups, send, 0)

            @pl.when(i > 0)
            def _():
                lax.fori_loop(0, groups, send, 0)

            return c

        lax.fori_loop(0, lines, line, 0)
        return carry

    lax.fori_loop(0, components, solve, 0)

    def finish(v, carry):
        others = pl.ds(0, devices - 1)
        pltpu.make_async_copy(sent_ref.at[v, others], sent_ref.at[v, others], send_one.at[v]).wait()
        pltpu.make_async_copy(done.at[v, others], done.at[v, others], send_two.at[v]).wait()
        pltpu.make_async_copy(back_ref.at[v], back_ref.at[v], recv_two.at[v]).wait()
        return carry

    lax.fori_loop(0, components, finish, 0)


def middle(inverse_z, high, low, early, sent, groups, lines):
    components, devices, depth, columns, rows = sent.shape
    total_y = high.shape[0]
    total_z = groups * 2 * depth
    whole = (components, devices, 2 * depth, columns, rows)
    return pl.pallas_call(
        functools.partial(middle_body, groups, lines),
        in_specs=[
            pl.BlockSpec(memory_space=pltpu.SMEM),
            pl.BlockSpec(memory_space=pltpu.VMEM),
            pl.BlockSpec(memory_space=pltpu.VMEM),
            pl.BlockSpec(memory_space=pl.ANY),
            pl.BlockSpec(memory_space=pl.ANY),
        ],
        out_specs=pl.BlockSpec(memory_space=pl.ANY),
        out_shape=jax.ShapeDtypeStruct(whole, jnp.float32),
        scratch_shapes=[
            pltpu.VMEM(sent.shape, jnp.float32),
            pltpu.VMEM(sent.shape, jnp.float32),
            pltpu.VMEM(whole, jnp.float32),
            pltpu.VMEM((total_z * columns, total_y), jnp.bfloat16),
            pltpu.VMEM((total_z * columns, total_y), jnp.bfloat16),
            pltpu.VMEM((total_z, columns, rows), jnp.float32),
            pltpu.SemaphoreType.DMA,
            pltpu.SemaphoreType.DMA((components,)),
            pltpu.SemaphoreType.DMA((components,)),
            pltpu.SemaphoreType.DMA((components,)),
            pltpu.SemaphoreType.DMA((components,)),
        ],
        compiler_params=pltpu.CompilerParams(
            collective_id=0, has_side_effects=True, vmem_limit_bytes=48 * 2**20
        ),
    )(inverse_z, high, low, early, sent)


def turn_body(back_ref, out_ref):
    devices, depth, columns, rows = back_ref.shape[1:]
    for plane in range(depth):
        out_ref[0, plane] = back_ref[0, :, plane].reshape(devices * columns, rows).T


def turn(back):
    components, devices, depth, columns, rows = back.shape
    width = devices * columns
    return pl.pallas_call(
        turn_body,
        grid=(components,),
        in_specs=[pl.BlockSpec((1, devices, depth, columns, rows), lambda v: (v, 0, 0, 0, 0))],
        out_specs=pl.BlockSpec((1, depth, rows, width), lambda v: (v, 0, 0, 0)),
        out_shape=jax.ShapeDtypeStruct((components, depth, rows, width), jnp.float32),
        compiler_params=pltpu.CompilerParams(vmem_limit_bytes=32 * 2**20),
    )(back)


def shards_exchange(adjoint, source, jacobian, inverse_x, inverse_y, inverse_z):
    groups = lax.axis_size("grp")
    lines = lax.axis_size("line")
    count = lines - 1
    rows, depth = adjoint.shape[2], adjoint.shape[1]
    before = lax.ppermute(adjoint[:, :, rows - 8 :], "line", [(i, i + 1) for i in range(count)])
    after = lax.ppermute(adjoint[:, :, :8], "line", [(i + 1, i) for i in range(count)])
    below = lax.ppermute(adjoint[:, depth - 2 :], "grp", [(i, i + 1) for i in range(groups - 1)])
    head, below = lax.optimization_barrier((adjoint[:, :2], below))
    above = lax.ppermute(head, "grp", [(i + 1, i) for i in range(groups - 1)])
    split_x = split_halves(inverse_x)
    first = (below, adjoint, before, after)
    sent = residual_sweep(0, jacobian, *split_x, source, first, (), groups * lines)
    early = spread(sent, groups, lines)
    second = (adjoint, above, before, after)
    sent = residual_sweep(1, jacobian, *split_x, source, second, (early,), groups * lines)
    back = middle(inverse_z, *split_halves(inverse_y), early, sent, groups, lines)
    return turn(back)


def shards(adjoint, source, jacobian, inverse_x, inverse_y, inverse_z):
    devices = lax.axis_size("grp") * lax.axis_size("line")
    whole_tiles = adjoint.shape[2] % 128 == 0 and (adjoint.shape[3] // devices) % 16 == 0 and adjoint.shape[1] == 4
    chosen = shards_exchange if whole_tiles else shards_plain
    return chosen(adjoint, source, jacobian, inverse_x, inverse_y, inverse_z)


def solution(mesh):
    placed = (P(None, "grp", "line", None), P(None, "grp", "line", None), P(), P(), P(), P())
    return jax.shard_map(
        shards, mesh=mesh, in_specs=placed, out_specs=P(None, "grp", "line", None), check_vma=False
    )
```

```python
import functools

import jax
import jax.numpy as jnp
from jax import lax
from jax.experimental import pallas as pl
from jax.experimental.pallas import tpu as pltpu
from jax.sharding import PartitionSpec as P

dissipation = 0.05
highest = lax.Precision.HIGHEST


def padded_2(cells, sides, width):
    for axis, dim in sides:
        count = lax.axis_size(axis)
        ends = count - 1
        head = lax.slice_in_dim(cells, 0, width, axis=dim)
        tail = lax.slice_in_dim(cells, cells.shape[dim] - width, cells.shape[dim], axis=dim)
        cells = jnp.concatenate(
            [
                lax.ppermute(tail, axis, [(i, (i + 1) % count) for i in range(ends)]),
                cells,
                lax.ppermute(head, axis, [((i + 1) % count, i) for i in range(ends)]),
            ],
            axis=dim,
        )
    return cells


def shift_last(field, offset):
    if offset == 0:
        return field
    zeros = jnp.zeros(field.shape[:-1] + (abs(offset),), field.dtype)
    if offset > 0:
        return jnp.concatenate([field[..., offset:], zeros], axis=-1)
    return jnp.concatenate([zeros, field[..., :offset]], axis=-1)


def stencil_sum(padded, source, jacobian):
    components = source.shape[0]
    depth = source.shape[1]
    rows_local = source.shape[2]

    def window(step_z, step_y, step_x):
        inner = padded[:, 2 + step_z : 2 + step_z + depth, 2 + step_y : 2 + step_y + rows_local, :]
        return shift_last(inner, step_x)

    centre = window(0, 0, 0)
    units = ((1, 0, 0), (0, 1, 0), (0, 0, 1))
    damping = jnp.zeros_like(source)
    centrals = []
    for direction in range(3):
        step_z, step_y, step_x = units[direction]
        forward = window(step_z, step_y, step_x)
        backward = window(-step_z, -step_y, -step_x)
        far_forward = window(2 * step_z, 2 * step_y, 2 * step_x)
        far_backward = window(-2 * step_z, -2 * step_y, -2 * step_x)
        centrals.append(0.5 * (forward - backward))
        damping = damping + (
            far_forward - 4.0 * forward + 6.0 * centre - 4.0 * backward + far_backward
        )
    outputs = []
    for target in range(components):
        total = source[target]
        for direction in range(3):
            for anchor in range(components):
                total = total + jacobian[direction, anchor, target] * centrals[direction][anchor]
        outputs.append(total)
    return jnp.stack(outputs, axis=0) - dissipation * damping


def shards_plain(adjoint, source, jacobian, inverse_x, inverse_y, inverse_z):
    components = adjoint.shape[0]
    depth = adjoint.shape[1]
    rows_local = adjoint.shape[2]
    width = adjoint.shape[3]
    line_count = lax.axis_size("line")
    group_count = lax.axis_size("grp")
    total_y = inverse_y.shape[0]
    total_z = inverse_z.shape[0]
    padded = padded_2(adjoint, (("grp", 1), ("line", 2)), 2)
    residual = stencil_sum(padded, source, jacobian)
    flat = residual.reshape(components * depth * rows_local, width)
    swept = lax.dot_general(inverse_x, flat, (((1,), (1,)), ((), ())), precision=highest)
    block_x = width // line_count
    block_y = total_y // group_count
    sent = swept.reshape(line_count, block_x * components * depth * rows_local)
    lines = lax.all_to_all(sent, "line", split_axis=0, concat_axis=0, tiled=True)
    lines = lines.reshape(line_count, block_x * components * depth, rows_local)
    split_y = inverse_y.reshape(total_y, line_count, rows_local)
    along_y = lax.dot_general(lines, split_y, (((0, 2), (1, 2)), ((), ())), precision=highest)
    along_y = along_y.reshape(block_x * components, depth, group_count, block_y)
    columns = lax.all_to_all(along_y, "grp", split_axis=2, concat_axis=1, tiled=True)
    columns = columns.reshape(block_x * components, total_z, block_y)
    along_z = lax.dot_general(inverse_z, columns, (((1,), (1,)), ((), ())), precision=highest)
    regrouped = lax.all_to_all(along_z, "grp", split_axis=0, concat_axis=2, tiled=True)
    regrouped = regrouped.reshape(depth, block_x, components, line_count, rows_local)
    returned = lax.all_to_all(regrouped, "line", split_axis=3, concat_axis=1, tiled=True)
    returned = returned.reshape(depth, width, components, rows_local)
    return jnp.transpose(returned, (2, 0, 3, 1))


MESH = pl.DeviceIdType.MESH


def halves(values):
    high = values.astype(jnp.bfloat16)
    return high, (values - high.astype(jnp.float32)).astype(jnp.bfloat16)


def split_halves(values):
    high = lax.reduce_precision(values, exponent_bits=8, mantissa_bits=7)
    return high.astype(jnp.bfloat16), (values - high).astype(jnp.bfloat16)


def product(left, right):
    dims = (((1,), (1,)), ((), ()))

    def one(a, b):
        return lax.dot_general(a, b, dims, preferred_element_type=jnp.float32)

    return one(left[0], right[0]) + (one(left[0], right[1]) + one(left[1], right[0]))


def shift_x(field, offset, place):
    width = field.shape[-1]
    moved = pltpu.roll(field, (-offset) % width, axis=1)
    inside = place < width - offset if offset > 0 else place >= -offset
    return jnp.where(inside, moved, 0.0)


def residual_sweep_body(
    pair, jacobian_ref, high_ref, low_ref, source_ref, first_ref, second_ref, before_ref, after_ref, *rest

):
    out_ref, padded, residual, sems = rest[-4:]
    v = pl.program_id(0)
    components = first_ref.shape[0]
    depth, rows, width = source_ref.shape[1:]

    @pl.when(v == 0)
    def _():
        inner = pl.ds(2, depth)
        middle_rows = pl.ds(8, rows)
        cut = first_ref.shape[1]
        copies = [
            pltpu.make_async_copy(first_ref, padded.at[:, pl.ds(0, cut), middle_rows], sems.at[0]),
            pltpu.make_async_copy(
                second_ref, padded.at[:, pl.ds(cut, depth + 4 - cut), middle_rows], sems.at[1]
            ),
            pltpu.make_async_copy(
                before_ref.at[:, pl.ds(pair * depth, depth)], padded.at[:, inner, pl.ds(0, 8)], sems.at[2]
            ),
            pltpu.make_async_copy(
                after_ref.at[:, pl.ds(pair * depth, depth)],
                padded.at[:, inner, pl.ds(rows + 8, 8)],
                sems.at[3],
            ),
        ]
        for copy in copies:
            copy.start()
        for copy in copies:
            copy.wait()

    place = lax.broadcasted_iota(jnp.int32, (8, width), 1)
    row = lax.broadcasted_iota(jnp.int32, (8, width), 0)
    factors = [[0.5 * jacobian_ref[d, w, v] for w in range(components)] for d in range(3)]

    def plane(z):
        def read(w, dz, start):
            return padded[w, z + 2 + dz, pl.ds(start, 8), :]

        def along(start):
            total = factors[1][0] * read(0, 0, start)
            for w in range(1, components):
                total = total + factors[1][w] * read(w, 0, start)
            return total

        def tile(t, carry):
            behind, here = carry
            start = pl.multiple_of(t * 8, 8)
            at = pl.multiple_of(t * 8 + 8, 8)
            after = pl.multiple_of(t * 8 + 16, 8)
            ahead = along(after)
            total = source_ref[0, z, pl.ds(start, 8), :]
            across = factors[2][0] * read(0, 0, at)
            for w in range(1, components):
                across = across + factors[2][w] * read(w, 0, at)
            for w in range(components):
                total = total + factors[0][w] * (read(w, 1, at) - read(w, -1, at))
            centre, last, coming = read(v, 0, at), read(v, 0, start), read(v, 0, after)
            scale = 4.0 * dissipation
            total = total + scale * (read(v, 1, at) + read(v, -1, at))
            scaled = scale * centre
            forward = jnp.where(row == 0, scale * coming + ahead, scaled + here)
            backward = jnp.where(row == 7, scale * last - behind, scaled - here)
            total = total + pltpu.roll(forward, 7, axis=0) + pltpu.roll(backward, 1, axis=0)
            total = total + shift_x(scaled + across, 1, place) + shift_x(scaled - across, -1, place)
            far = read(v, 2, at) + read(v, -2, at)
            far = far + pltpu.roll(jnp.where(row < 2, coming, centre), 6, axis=0)
            far = far + pltpu.roll(jnp.where(row >= 6, last, centre), 2, axis=0)
            far = far + shift_x(centre, 2, place) + shift_x(centre, -2, place)
            total = total - dissipation * (far + 18.0 * centre)
            residual[pl.ds(pl.multiple_of(z * rows + start, 8), 8), :] = total
            return here, ahead

        lax.fori_loop(0, rows // 8, tile, (along(0), along(8)))

    for z in range(depth):
        plane(z)
    swept = product((high_ref[...], low_ref[...]), halves(residual[...]))
    for plane in range(depth):
        part = swept[:, plane * rows : (plane + 1) * rows]
        out_ref[0, :, plane] = part.reshape(out_ref.shape[1], out_ref.shape[3], rows)


def residual_sweep(pair, jacobian, high, low, source, parts, ahead, devices):
    components, depth, rows, width = source.shape
    depth = depth // 2
    columns = width // devices
    once = pl.Buffered(1)
    return pl.pallas_call(
        functools.partial(residual_sweep_body, pair),
        grid=(components,),
        in_specs=[
            pl.BlockSpec(memory_space=pltpu.SMEM),
            pl.BlockSpec((width, width), lambda v: (0, 0), pipeline_mode=once),
            pl.BlockSpec((width, width), lambda v: (0, 0), pipeline_mode=once),
            pl.BlockSpec((1, depth, rows, width), lambda v: (v, pair, 0, 0)),
        ]
        + [pl.BlockSpec(memory_space=pl.ANY)] * (len(parts) + len(ahead)),
        out_specs=pl.BlockSpec((1, devices, depth, columns, rows), lambda v: (v, 0, 0, 0, 0)),
        out_shape=jax.ShapeDtypeStruct((components, devices, depth, columns, rows), jnp.float32),
        scratch_shapes=[
            pltpu.VMEM((components, depth + 4, rows + 16, width), jnp.float32),
            pltpu.VMEM((depth * rows, width), jnp.float32),
            pltpu.SemaphoreType.DMA((4,)),
        ],
        compiler_params=pltpu.CompilerParams(vmem_limit_bytes=48 * 2**20),
    )(jacobian, high, low, source, *parts, *ahead)


def meet(groups, lines):
    devices = groups * lines
    own_g = lax.axis_index("grp")
    own_l = lax.axis_index("line")

    def partner(step):
        l = lax.rem(own_l + step // groups, lines)
        g = lax.rem(own_g + step % groups, groups)
        return g, l

    barrier = pltpu.get_barrier_semaphore()

    def greet(step, carry):
        g, l = partner(step)
        pl.semaphore_signal(barrier, inc=1, device_id=(g, l), device_id_type=MESH)
        return carry

    lax.fori_loop(1, devices, greet, 0)
    pl.semaphore_wait(barrier, devices - 1)
    return own_g, own_l, partner


def sweep_spread_body(groups, lines, *refs):
    inputs, got_ref = refs[:8], refs[8]
    padded, residual, sems, sent, send_sem, recv_sem = refs[9:]
    components, devices = sent.shape[:2]
    v = pl.program_id(0)
    own_g = lax.axis_index("grp")
    own_l = lax.axis_index("line")
    own = own_g * lines + own_l

    @pl.when(v == 0)
    def _():
        meet(groups, lines)

    residual_sweep_body(0, *inputs, sent.at[pl.ds(v, 1)], padded, residual, sems)
    pltpu.make_async_copy(sent.at[v, own], got_ref.at[v, own], recv_sem).start()

    def one(step, c):
        l = lax.rem(own_l + step // groups, lines)
        g = lax.rem(own_g + step % groups, groups)
        pltpu.make_async_remote_copy(
            src_ref=sent.at[v, g * lines + l],
            dst_ref=got_ref.at[v, own],
            send_sem=send_sem,
            recv_sem=recv_sem,
            device_id=(g, l),
            device_id_type=MESH,
        ).start()
        return c

    lax.fori_loop(1, devices, one, 0)

    @pl.when(v == components - 1)
    def _():
        others = sent.at[:, pl.ds(0, devices - 1)]
        pltpu.make_async_copy(others, others, send_sem).wait()
        pltpu.make_async_copy(got_ref, got_ref, recv_sem).wait()


def sweep_spread(jacobian, high, low, source, parts, groups, lines):
    components, depth, rows, width = source.shape
    depth = depth // 2
    devices = groups * lines
    shape = (components, devices, depth, width // devices, rows)
    once = pl.Buffered(1)
    return pl.pallas_call(
        functools.partial(sweep_spread_body, groups, lines),
        grid=(components,),
        in_specs=[
            pl.BlockSpec(memory_space=pltpu.SMEM),
            pl.BlockSpec((width, width), lambda v: (0, 0), pipeline_mode=once),
            pl.BlockSpec((width, width), lambda v: (0, 0), pipeline_mode=once),
            pl.BlockSpec((1, depth, rows, width), lambda v: (v, 0, 0, 0)),
        ]
        + [pl.BlockSpec(memory_space=pl.ANY)] * len(parts),
        out_specs=pl.BlockSpec(memory_space=pl.ANY),
        out_shape=jax.ShapeDtypeStruct(shape, jnp.float32),
        scratch_shapes=[
            pltpu.VMEM((components, depth + 4, rows + 16, width), jnp.float32),
            pltpu.VMEM((depth * rows, width), jnp.float32),
            pltpu.SemaphoreType.DMA((4,)),
            pltpu.VMEM(shape, jnp.float32),
            pltpu.SemaphoreType.DMA,
            pltpu.SemaphoreType.DMA,
        ],
        cost_estimate=pl.CostEstimate(flops=10**11, bytes_accessed=10**8, transcendentals=0),
        compiler_params=pltpu.CompilerParams(
            collective_id=1, has_side_effects=True, vmem_limit_bytes=48 * 2**20
        ),
    )(jacobian, high, low, source, *parts)


def middle_body(
    groups, lines, z_ref, high_ref, low_ref, early_ref, sent_ref, back_ref,
    early, got, done, field_high, field_low, lined, early_sem, send_one, recv_one, send_two, recv_two,
):
    components, devices, depth, columns, rows = sent_ref.shape
    total_z = groups * 2 * depth
    own_g, own_l, partner = meet(groups, lines)
    own = own_g * lines + own_l
    fetch = pltpu.make_async_copy(early_ref, early, early_sem)
    fetch.start()

    def first(v, carry):
        pltpu.make_async_copy(sent_ref.at[v, own], got.at[v, own], recv_one.at[v]).start()

        def one(step, c):
            g, l = partner(step)
            pltpu.make_async_remote_copy(
                src_ref=sent_ref.at[v, g * lines + l],
                dst_ref=got.at[v, own],
                send_sem=send_one.at[v],
                recv_sem=recv_one.at[v],
                device_id=(g, l),
                device_id_type=MESH,
            ).start()
            return c

        lax.fori_loop(1, devices, one, 0)
        return carry

    lax.fori_loop(0, components, first, 0)
    fetch.wait()

    def solve(v, carry):
        pltpu.make_async_copy(got.at[v], got.at[v], recv_one.at[v]).wait()
        for g in range(groups):
            for place, half in enumerate((early, got)):
                block = jnp.concatenate(
                    [half[v, g * lines + l].reshape(depth * columns, rows) for l in range(lines)],
                    axis=-1,
                )
                high, low = halves(block)
                at = pl.ds((2 * g + place) * depth * columns, depth * columns)
                field_high[at, :] = high
                field_low[at, :] = low

        def line(i, c):
            l = lax.rem(own_l + i, lines)
            at = pl.ds(pl.multiple_of(l * rows, rows), rows)
            solved = product(
                (field_high[...], field_low[...]), (high_ref[at, :], low_ref[at, :])
            )
            lined[...] = solved.reshape(total_z, columns, rows)
            for q in range(total_z):
                total = z_ref[q, 0] * lined[0]
                for z in range(1, total_z):
                    total = total + z_ref[q, z] * lined[z]
                done[v, (q // (2 * depth)) * lines + l, q % (2 * depth)] = total

            def send(j, cc):
                g = lax.rem(own_g + j, groups)
                pltpu.make_async_remote_copy(
                    src_ref=done.at[v, g * lines + l],
                    dst_ref=back_ref.at[v, own],
                    send_sem=send_two.at[v],
                    recv_sem=recv_two.at[v],
                    device_id=(g, l),
                    device_id_type=MESH,
                ).start()
                return cc

            @pl.when(i == 0)
            def _():
                pltpu.make_async_copy(done.at[v, own], back_ref.at[v, own], recv_two.at[v]).start()
                lax.fori_loop(1, groups, send, 0)

            @pl.when(i > 0)
            def _():
                lax.fori_loop(0, groups, send, 0)

            return c

        lax.fori_loop(0, lines, line, 0)
        return carry

    lax.fori_loop(0, components, solve, 0)

    def finish(v, carry):
        others = pl.ds(0, devices - 1)
        pltpu.make_async_copy(sent_ref.at[v, others], sent_ref.at[v, others], send_one.at[v]).wait()
        pltpu.make_async_copy(done.at[v, others], done.at[v, others], send_two.at[v]).wait()
        pltpu.make_async_copy(back_ref.at[v], back_ref.at[v], recv_two.at[v]).wait()
        return carry

    lax.fori_loop(0, components, finish, 0)


def middle(inverse_z, high, low, early, sent, groups, lines):
    components, devices, depth, columns, rows = sent.shape
    total_y = high.shape[0]
    total_z = groups * 2 * depth
    whole = (components, devices, 2 * depth, columns, rows)
    return pl.pallas_call(
        functools.partial(middle_body, groups, lines),
        in_specs=[
            pl.BlockSpec(memory_space=pltpu.SMEM),
            pl.BlockSpec(memory_space=pltpu.VMEM),
            pl.BlockSpec(memory_space=pltpu.VMEM),
            pl.BlockSpec(memory_space=pl.ANY),
            pl.BlockSpec(memory_space=pl.ANY),
        ],
        out_specs=pl.BlockSpec(memory_space=pl.ANY),
        out_shape=jax.ShapeDtypeStruct(whole, jnp.float32),
        scratch_shapes=[
            pltpu.VMEM(sent.shape, jnp.float32),
            pltpu.VMEM(sent.shape, jnp.float32),
            pltpu.VMEM(whole, jnp.float32),
            pltpu.VMEM((total_z * columns, total_y), jnp.bfloat16),
            pltpu.VMEM((total_z * columns, total_y), jnp.bfloat16),
            pltpu.VMEM((total_z, columns, rows), jnp.float32),
            pltpu.SemaphoreType.DMA,
            pltpu.SemaphoreType.DMA((components,)),
            pltpu.SemaphoreType.DMA((components,)),
            pltpu.SemaphoreType.DMA((components,)),
            pltpu.SemaphoreType.DMA((components,)),
        ],
        compiler_params=pltpu.CompilerParams(
            collective_id=0, has_side_effects=True, vmem_limit_bytes=48 * 2**20
        ),
    )(inverse_z, high, low, early, sent)


def turn_body(back_ref, out_ref):
    devices, depth, columns, rows = back_ref.shape[1:]
    for plane in range(depth):
        out_ref[0, plane] = back_ref[0, :, plane].reshape(devices * columns, rows).T


def turn(back):
    components, devices, depth, columns, rows = back.shape
    width = devices * columns
    return pl.pallas_call(
        turn_body,
        grid=(components,),
        in_specs=[pl.BlockSpec((1, devices, depth, columns, rows), lambda v: (v, 0, 0, 0, 0))],
        out_specs=pl.BlockSpec((1, depth, rows, width), lambda v: (v, 0, 0, 0)),
        out_shape=jax.ShapeDtypeStruct((components, depth, rows, width), jnp.float32),
        compiler_params=pltpu.CompilerParams(vmem_limit_bytes=32 * 2**20),
    )(back)


def shards_exchange(adjoint, source, jacobian, inverse_x, inverse_y, inverse_z):
    groups = lax.axis_size("grp")
    lines = lax.axis_size("line")
    count = lines - 1
    rows, depth = adjoint.shape[2], adjoint.shape[1]
    before = lax.ppermute(adjoint[:, :, rows - 8 :], "line", [(i, i + 1) for i in range(count)])
    after = lax.ppermute(adjoint[:, :, :8], "line", [(i + 1, i) for i in range(count)])
    below = lax.ppermute(adjoint[:, depth - 2 :], "grp", [(i, i + 1) for i in range(groups - 1)])
    head, below = lax.optimization_barrier((adjoint[:, :2], below))
    above = lax.ppermute(head, "grp", [(i + 1, i) for i in range(groups - 1)])
    split_x = split_halves(inverse_x)
    first = (below, adjoint, before, after)
    early = sweep_spread(jacobian, *split_x, source, first, groups, lines)
    second = (adjoint, above, before, after)
    sent = residual_sweep(1, jacobian, *split_x, source, second, (early,), groups * lines)
    back = middle(inverse_z, *split_halves(inverse_y), early, sent, groups, lines)
    return turn(back)


def shards(adjoint, source, jacobian, inverse_x, inverse_y, inverse_z):
    devices = lax.axis_size("grp") * lax.axis_size("line")
    whole_tiles = adjoint.shape[2] % 128 == 0 and (adjoint.shape[3] // devices) % 16 == 0 and adjoint.shape[1] == 4
    chosen = shards_exchange if whole_tiles else shards_plain
    return chosen(adjoint, source, jacobian, inverse_x, inverse_y, inverse_z)


def solution(mesh):
    placed = (P(None, "grp", "line", None), P(None, "grp", "line", None), P(), P(), P(), P())
    return jax.shard_map(
        shards, mesh=mesh, in_specs=placed, out_specs=P(None, "grp", "line", None), check_vma=False
    )
```
